32 devices in a mesh: dp: 16 (over z, y, x), cuts: 2 (over core).
Axes of the slice: x: 2, y: 2, z: 4, core: 2. Of those that a mesh axis runs over, the one named last changes fastest.
Arguments:
- queries: bfloat16 [128, 2048], P('dp', 'cuts'), may hold values from -240 to 240
- new_keys: bfloat16 [128, 2048], P('dp', 'cuts'), may hold values from -6 to 6
- new_values: bfloat16 [128, 2048], P('dp', 'cuts'), may hold values from -6 to 6
- key_cache: bfloat16 [128, 64, 2048], P('dp', None, 'cuts'), may hold values from -6 to 6
- value_cache: bfloat16 [128, 64, 2048], P('dp', None, 'cuts'), may hold values from -6 to 6
- lengths: int32 [128], P('dp'), may hold values from 1 to 64
- resid: bfloat16 [128, 2048], P('dp'), may hold values from -6 to 6
- norm_gain: float32 [2048], replicated, may hold values from 0.5 to 1.5
- w_out: bfloat16 [2048, 2048], P('cuts'), may hold values from -0.125 to 0.125
- experts: int32 [128, 1], P('dp'), may hold values from 0 to 3; in each aligned block of 8 rows (0 to 7, 8 to 15, ...) at most 4 rows name the same one
- w_up: bfloat16 [16, 2048, 2048], P('dp', None, 'cuts'), may hold values from -0.125 to 0.125
- w_down: bfloat16 [16, 2048, 2048], P('dp', 'cuts'), may hold values from -0.0625 to 0.0625
Outputs:
- mixed: bfloat16 [128, 2048], P('dp', 'cuts')
The draws below stay inside these ranges and needn't reach their ends.
Inputs may be any that keep to these rules, and one draw needn't show every extreme that they name: `experts`: among the 8 rows of one dp index each expert is named by at most 4 rows, and by exactly 4 in some.
All inputs are finite; a program needn't handle non-finite values.
Results may differ from the reference program's by a relative error of at most 0.014.
Values may be sent and summed in bfloat16 or wider, within the bound.
A program may use at most 64 MiB of HBM per device.

```python
import math
import jax
import jax.numpy as jnp
import numpy as np
from jax import lax

D = 2048
HEADS = 16
HD = 128
FF = 8192
GROUP = 4
ROWS = 8
LEN = 64
EXPERTS = 4
CAP = 4
TOKENS = 128
N_DP = 16
N_CUTS = 2


def draw_queries(key, part):
    key = jax.random.fold_in(key, 11)
    base = jax.random.truncated_normal(key, -6.0, 6.0, (TOKENS, HEADS * HD), jnp.float32)
    return base.astype(jnp.bfloat16)


def place_ends(values, stream_key, smallest, high):
    dims = values.shape
    place = [jax.random.randint(jax.random.fold_in(stream_key, axis), (), 0, dims[axis]) for axis in range(len(dims))]
    values = values.at[tuple(place)].set(smallest)
    longest = dims.index(max(dims))
    place[longest] = (place[longest] + 1) % dims[longest]
    return values.at[tuple(place)].set(high)


def block_levels(stream_key, shape, cuts, least, largest):
    factor_of = 1.0
    for dim, shards_of in cuts:
        steps = jax.random.uniform(jax.random.fold_in(jax.random.fold_in(stream_key, 6), dim), (shards_of,), jnp.float32, least / len(cuts), largest / len(cuts))
        factor_of = factor_of * jnp.repeat(jnp.exp(steps), shape[dim] // shards_of).reshape((-1,) + (1,) * (len(shape) - 1 - dim))
    return factor_of


def deal_out(stream_key, own, number, rows, number_of, top, bound, slope):
    sequence = jax.random.permutation(stream_key, number_of)
    packed, usual = load_shares(number_of, rows * top, bound, slope, True), load_shares(number_of, rows * top, bound, slope, False)
    places = jnp.arange(number_of)

    def named(tallies, offset_by):
        used = int((tallies > 0).sum())
        fixed = max(1, used // 4)
        passed = fixed + (places - fixed + offset_by * (used - fixed)) % max(1, number_of - fixed)
        return jnp.zeros((number_of,), jnp.int32).at[sequence[jnp.where(places < fixed, places, passed)]].set(jnp.asarray(tallies, jnp.int32))

    tallies = jnp.where(number % 4 == 0, named(packed, number // 4), named(usual, number - number // 4 - 1))
    mixed = jax.random.permutation(jax.random.fold_in(own, 3), number_of)
    giver, sink = mixed[0:number_of // 2 * 2:2], mixed[1:number_of // 2 * 2:2]
    margin = jnp.minimum(tallies[giver] - 1, bound - tallies[sink]) // 2
    margin = jnp.where((giver == sequence[0]) | (sink == sequence[0]) | (tallies[sink] == 0), 0, jnp.maximum(margin, 0))
    passed = jax.random.randint(jax.random.fold_in(own, 4), (number_of // 2,), 0, 1 << 20) % (margin + 1)
    tallies = tallies.at[giver].add(-passed).at[sink].add(passed)
    members = jnp.searchsorted(jnp.cumsum(tallies), jnp.arange(rows * top), side="right").astype(jnp.int32)
    table = members.reshape(top, rows).T
    table = table[jax.random.permutation(jax.random.fold_in(own, 1), rows)]
    offset_by = jax.random.randint(jax.random.fold_in(own, 2), (rows, 1), 0, top)
    return jnp.take_along_axis(table, (jnp.arange(top)[None, :] + offset_by) % top, axis=1)


def load_shares(number_of, total, reach, slope, full):
    loads = [(1 << 20) // math.isqrt(standing ** slope) + 1 for standing in range(1, number_of + 1)]
    largest = reach if full else min(reach, max(-(-total // number_of), total * loads[0] // sum(loads)))
    least = 1 if total - largest >= number_of - 1 else 0
    holding, spare = [largest] + [least] * (number_of - 1), total - largest - least * (number_of - 1)
    while spare > 0:
        movable = [i for i in range(1, number_of) if holding[i] < largest] or [i for i in range(1, number_of) if holding[i] < reach]
        whole, remaining = sum([loads[i] for i in movable]), spare
        for i in movable:
            addition = min(reach - holding[i], max(1, remaining * loads[i] // whole), spare)
            holding[i] = holding[i] + addition
            spare = spare - addition
    return np.array(holding)


def scatter_about(rng, shape, deviation, limit, shards=(), kind=jnp.bfloat16):
    values = jax.random.normal(rng, shape, jnp.float32) * deviation
    if len(shards) > 0:
        values = block_levels(rng, shape, shards, -0.22, 0.18) * values
    return jnp.clip(values, min=-limit, max=limit).astype(kind)


def setup_inputs(seed: int = 0) -> dict:
    key_list = jax.random.split(jax.random.key(seed), 13)
    queries = draw_queries(jax.random.fold_in(key_list[12], 71), 0)
    new_keys = scatter_about(key_list[1], (TOKENS, HEADS * HD), 1.0, 6.0, ((0, 16), (1, 2)))
    new_values = scatter_about(key_list[2], (TOKENS, HEADS * HD), 1.0, 6.0, ((0, 16), (1, 2)))
    key_cache = scatter_about(key_list[3], (TOKENS, LEN, HEADS * HD), 1.0, 6.0, ((0, 16), (2, 2)))
    value_cache = scatter_about(key_list[4], (TOKENS, LEN, HEADS * HD), 1.0, 6.0, ((0, 16), (2, 2)))
    lengths = place_ends(jax.random.randint(key_list[5], (TOKENS,), 1, LEN + 1), jax.random.fold_in(key_list[5], 1), 1, LEN).astype(jnp.int32)
    resid = scatter_about(key_list[6], (TOKENS, D), 1.0, 6.0, ((0, 16),))
    norm_gain = jnp.clip(1.0 + 0.1 * jax.random.normal(key_list[7], (D,), jnp.float32), 0.5, 1.5)
    w_out = scatter_about(key_list[8], (HEADS * HD, D), (HEADS * HD) ** -0.5, 0.125, ((0, 2),))
    experts_keys = jax.random.split(jax.random.fold_in(key_list[9], 1), TOKENS // ROWS)
    experts_turns = jax.random.permutation(jax.random.fold_in(key_list[9], 3), TOKENS // ROWS)
    experts = jax.vmap(lambda own, number: deal_out(jax.random.fold_in(key_list[9], 2), own, number, ROWS, EXPERTS, 1, CAP, 2))(experts_keys, experts_turns).reshape((TOKENS, 1))
    w_up = scatter_about(key_list[10], (EXPERTS * GROUP, D, FF // GROUP), D ** -0.5, 0.125, ((0, 16), (2, 2)))
    w_down = scatter_about(key_list[11], (EXPERTS * GROUP, FF // GROUP, D), FF ** -0.5, 0.0625, ((0, 16), (1, 2)))
    return dict(queries=queries, new_keys=new_keys, new_values=new_values, key_cache=key_cache, value_cache=value_cache, lengths=lengths, resid=resid, norm_gain=norm_gain, w_out=w_out, experts=experts, w_up=w_up, w_down=w_down)


def attend(block):
    query, nkey, nval, kcache, vcache, valid_len = block
    count = query.shape[0]
    scale = 1.0 / HD ** 0.5
    qf = query.astype(jnp.float32).reshape(count, HEADS, HD)
    kf = kcache.astype(jnp.float32).reshape(count, LEN, HEADS, HD)
    vf = vcache.astype(jnp.float32).reshape(count, LEN, HEADS, HD)
    nk = nkey.astype(jnp.float32).reshape(count, HEADS, HD)
    nv = nval.astype(jnp.float32).reshape(count, HEADS, HD)
    scores = jnp.einsum('rhd,rjhd->rhj', qf, kf) * scale
    keep = jnp.arange(LEN)[None, None, :] < valid_len[:, None, None]
    scores = jnp.where(keep, scores, -1e+30)
    fresh = lax.optimization_barrier(jnp.sum(qf * nk, axis=-1)) * scale
    peak = jnp.maximum(lax.optimization_barrier(jnp.max(scores, axis=-1)), fresh)
    pcache = jnp.where(keep, jnp.exp(scores - peak[..., None]), 0.0)
    pnew = jnp.exp(fresh - peak)
    total = lax.optimization_barrier(jnp.sum(pcache, axis=-1)) + pnew
    pcache = (pcache / total[..., None]).astype(jnp.bfloat16)
    pnew = (pnew / total).astype(jnp.bfloat16)
    summed = jnp.einsum('rhj,rjhd->rhd', pcache.astype(jnp.float32), vf)
    summed = summed + pnew.astype(jnp.float32)[..., None] * nv
    return summed.reshape(count, HEADS * HD).astype(jnp.bfloat16)

def reference(queries, new_keys, new_values, key_cache, value_cache, lengths, resid, norm_gain, w_out, experts, w_up, w_down):
    blocks = (queries.reshape(N_DP, ROWS, HEADS * HD), new_keys.reshape(N_DP, ROWS, HEADS * HD), new_values.reshape(N_DP, ROWS, HEADS * HD), key_cache.reshape(N_DP, ROWS, LEN, HEADS * HD), value_cache.reshape(N_DP, ROWS, LEN, HEADS * HD), lengths.reshape(N_DP, ROWS))
    heads_out = lax.map(attend, blocks).reshape(TOKENS, HEADS * HD)
    attn = jnp.dot(heads_out, w_out, preferred_element_type=jnp.float32)
    hidden = resid.astype(jnp.float32) + attn
    meansq = lax.optimization_barrier(jnp.mean(hidden * hidden, axis=-1))
    normed = (hidden * lax.rsqrt(meansq + 1e-06)[:, None] * norm_gain[None, :]).astype(jnp.bfloat16)
    ids = experts[:, 0]
    slots_all = CAP * N_DP
    block_units = FF // GROUP // N_CUTS

    def one_expert(carry, expert):
        order = jnp.argsort((ids != expert).astype(jnp.int32), stable=True)[:slots_all].astype(jnp.int32)
        chosen = ids[order] == expert
        picked = normed[order]
        total = jnp.zeros((slots_all, D), jnp.float32)
        for group_idx in range(GROUP):
            upper = w_up[expert * GROUP + group_idx]
            lower = w_down[expert * GROUP + group_idx]
            act = jax.nn.gelu(jnp.dot(picked, upper, preferred_element_type=jnp.float32)).astype(jnp.bfloat16)
            part = jnp.zeros((slots_all, D), jnp.float32)
            for cut_idx in range(N_CUTS):
                lo_unit = cut_idx * block_units
                piece = jnp.dot(act[:, lo_unit:lo_unit + block_units], lower[lo_unit:lo_unit + block_units], preferred_element_type=jnp.float32).astype(jnp.bfloat16)
                part = part + lax.optimization_barrier(piece).astype(jnp.float32)
            rounded = lax.optimization_barrier(part.astype(jnp.bfloat16))
            total = total + rounded.astype(jnp.float32)
        carry = carry.at[order].add(jnp.where(chosen[:, None], total, 0.0))
        return (carry, None)
    expert_out, unused = lax.scan(one_expert, jnp.zeros((TOKENS, D), jnp.float32), jnp.arange(EXPERTS, dtype=jnp.int32))
    return (hidden + expert_out).astype(jnp.bfloat16)
```

```python
import functools

import jax
import jax.numpy as jnp
from jax import lax
from jax.experimental import pallas as pl
from jax.experimental.pallas import tpu as pltpu
from jax.sharding import PartitionSpec as P

HD = 128
GROUP = 4
TILE = 16
MESH = pl.DeviceIdType.MESH
F32 = jnp.float32
BF16 = jnp.bfloat16


def iota(shape, dim):
    return lax.broadcasted_iota(jnp.int32, shape, dim)


def div(x, n):
    return x >> (n.bit_length() - 1)


def mod(x, n):
    return x & (n - 1)


def one_hot(flags):
    return jnp.where(flags, 1.0, 0.0).astype(BF16)


def mm(a, b):
    return jnp.dot(a, b, preferred_element_type=F32)


def kernel(
    n_data,
    n_cuts,
    lengths,
    experts,
    q_hbm,
    nk_hbm,
    nv_hbm,
    k_hbm,
    v_hbm,
    resid_hbm,
    gain_hbm,
    wout_hbm,
    wup_hbm,
    wdown_hbm,
    out_ref,
    q_ref,
    nk_ref,
    nv_ref,
    k_ref,
    v_ref,
    resid_ref,
    gain_ref,
    wout_ref,
    wup_ref,
    wdown_ref,
    parts,
    hid_ref,
    packed,
    gath,
    mine,
    halves,
    share,
    red,
    going,
    back,
    load_sem,
    part_send,
    part_recv,
    z_send,
    z_recv,
    spread_send,
    spread_recv,
    half_send,
    half_recv,
    red_send,
    red_recv,
    back_send,
    back_recv,
):
    dp = lax.axis_index("dp")
    cut = lax.axis_index("cuts")
    me = dp // GROUP
    g = lax.rem(dp, GROUP)
    n_e = n_data // GROUP
    count, feats = q_ref.shape
    width_all = resid_ref.shape[1]
    width = width_all // n_cuts
    heads = feats // HD
    length = k_hbm.shape[1]
    slots = max(2, 2 * count * GROUP // n_data)
    scale = 1.0 / HD**0.5

    loads = [
        pltpu.make_async_copy(src, dst, load_sem.at[i])
        for i, (src, dst) in enumerate(
            (
                (q_hbm, q_ref),
                (nk_hbm, nk_ref),
                (k_hbm, k_ref),
                (nv_hbm, nv_ref),
                (v_hbm, v_ref),
                (resid_hbm, resid_ref),
                (gain_hbm, gain_ref),
                (wout_hbm, wout_ref),
                (wup_hbm.at[0], wup_ref),
                (wdown_hbm.at[0], wdown_ref),
            )
        )
    ]
    for load in loads:
        load.start()

    cut_peers = [lax.rem(cut + d, n_cuts) for d in range(1, n_cuts)]
    e_peers = [lax.rem(me + d, n_e) for d in range(1, n_e)]
    g_peers = [lax.rem(g + d, GROUP) for d in range(1, GROUP)]
    ids = [(dp, c) for c in cut_peers]
    ids += [(e * GROUP + g, cut) for e in e_peers]
    ids += [(me * GROUP + h, cut) for h in g_peers]
    barrier = pltpu.get_barrier_semaphore()
    for device in ids:
        pl.semaphore_signal(barrier, inc=1, device_id=device, device_id_type=MESH)

    def remote(src, dst, send, recv, device):
        return pltpu.make_async_remote_copy(
            src_ref=src, dst_ref=dst, send_sem=send, recv_sem=recv, device_id=device, device_id_type=MESH
        )

    sent = []

    pairs = count * heads
    spread_rows = one_hot(div(iota((pairs, count), 0), heads) == iota((pairs, count), 1))
    own_head = div(iota((pairs, feats), 1), HD) == mod(iota((pairs, feats), 0), heads)
    loads[0].wait()
    q_wide = jnp.where(own_head, mm(spread_rows, q_ref[...]), 0.0).astype(BF16)
    nt = (((1,), (1,)), ((), ()))
    loads[1].wait()
    fresh_all = lax.dot_general(q_wide, nk_ref[...], nt, preferred_element_type=F32)
    own_new = div(iota((pairs, count), 0), heads) == iota((pairs, count), 1)
    fresh = jnp.sum(jnp.where(own_new, fresh_all, 0.0), axis=1, keepdims=True) * scale
    loads[2].wait()
    span = count * length
    keys = k_ref[...].reshape(span, feats)
    scores = lax.dot_general(q_wide, keys, nt, preferred_element_type=F32) * scale
    col = iota((1, span), 1)
    limit = jnp.zeros((1, span), jnp.int32)
    for t in range(count):
        limit = jnp.where(div(col, length) == t, lengths[t], limit)
    valid = jnp.where(mod(col, length) < limit, div(col, length), -1)
    keep = div(iota((pairs, span), 0), heads) == valid
    scores = jnp.where(keep, scores, -1e30)
    peak = jnp.maximum(jnp.max(scores, axis=1, keepdims=True), fresh)
    pcache = jnp.where(keep, jnp.exp(scores - peak), 0.0)
    pnew = jnp.exp(fresh - peak)
    total = jnp.sum(pcache, axis=1, keepdims=True) + pnew
    pcache = (pcache / total).astype(BF16)
    pnew = (pnew / total).astype(BF16).astype(F32)
    loads[3].wait()
    new_rows = mm(spread_rows, nv_ref[...])
    loads[4].wait()
    summed = mm(pcache, v_ref[...].reshape(span, feats)) + pnew * new_rows
    summed = jnp.where(own_head, summed, 0.0).astype(BF16)
    join_rows = one_hot(div(iota((count, pairs), 1), heads) == iota((count, pairs), 0))
    heads_out = mm(join_rows, summed).astype(BF16)

    loads[7].wait()
    parts[cut] = mm(heads_out, wout_ref[...])
    pl.semaphore_wait(barrier, len(ids))
    for i, c in enumerate(cut_peers):
        copy = remote(parts.at[cut], parts.at[cut], part_send.at[i], part_recv.at[cut], (dp, c))
        copy.start()
        sent.append(copy)

    ids_of = [experts[t] for t in range(count)]
    place = []
    for t in range(count):
        slot = jnp.int32(0)
        for u in range(t):
            slot = slot + jnp.where(ids_of[u] == ids_of[t], 1, 0)
        place.append(ids_of[t] * slots + slot)
    nk = TILE // slots
    chunk = width_all // nk
    table_shape = (n_e * TILE, nk * count)
    row, col = iota(table_shape, 0), iota(table_shape, 1)
    target = jnp.zeros(table_shape, jnp.int32)
    for t in range(count):
        target = jnp.where(mod(col, count) == t, place[t], target)
    pack = one_hot(
        (div(mod(row, TILE), slots) == div(col, count))
        & (div(row, TILE) * slots + mod(row, slots) == target)
    )
    loads[5].wait()
    loads[6].wait()
    for c in cut_peers:
        remote(parts.at[c], parts.at[c], part_send.at[0], part_recv.at[c], (dp, c)).wait_recv()
    attn = parts[0]
    for c in range(1, n_cuts):
        attn = attn + parts[c]
    hidden = resid_ref[...].astype(F32) + attn
    hid_ref[...] = hidden
    meansq = jnp.mean(hidden * hidden, axis=1, keepdims=True)
    normed = hidden * lax.rsqrt(meansq + 1e-06) * gain_ref[...]
    stacked = jnp.concatenate([normed[:, k * chunk : (k + 1) * chunk] for k in range(nk)], axis=0)
    rows = mm(pack, stacked.astype(BF16)).astype(BF16)
    packed[...] = rows.reshape(n_e, TILE, chunk)

    for i, e in enumerate(e_peers):
        copy = remote(
            packed.at[e], gath.at[g, me], z_send.at[i], z_recv.at[me], (e * GROUP + g, cut)
        )
        copy.start()
        sent.append(copy)
    gath[g, me] = packed[me]
    for i, e in enumerate([me] + e_peers):
        if i > 0:
            remote(
                packed.at[e], gath.at[g, e], z_send.at[i - 1], z_recv.at[e], (e * GROUP + g, cut)
            ).wait_recv()
        for j, h in enumerate(g_peers):
            copy = remote(
                gath.at[g, e],
                gath.at[g, e],
                spread_send.at[j, i],
                spread_recv.at[g, e],
                (me * GROUP + h, cut),
            )
            copy.start()
            sent.append(copy)
    all_rows = GROUP * n_e * slots
    per_group = n_e * slots
    wide = GROUP * n_e * TILE
    row, col = iota((nk * all_rows, wide), 0), iota((nk * all_rows, wide), 1)
    which, m = div(row, all_rows), mod(row, all_rows)
    unpack = one_hot(col == div(m, slots) * TILE + which * slots + mod(m, slots))
    for i, e in enumerate([me] + e_peers):
        for j, h in enumerate(g_peers):
            remote(
                gath.at[h, e],
                gath.at[h, e],
                spread_send.at[j, i],
                spread_recv.at[h, e],
                (me * GROUP + h, cut),
            ).wait_recv()
    arrived = mm(unpack, gath[...].reshape(wide, chunk)).astype(BF16)
    loads[8].wait()
    up = mm(arrived[0:all_rows], wup_ref[0:chunk, :])
    for k in range(1, nk):
        up = up + mm(
            arrived[k * all_rows : (k + 1) * all_rows], wup_ref[k * chunk : (k + 1) * chunk, :]
        )
    act = jax.nn.gelu(up).astype(BF16)

    loads[9].wait()
    for i, c in enumerate(cut_peers + [cut]):
        columns = pl.ds(pl.multiple_of(c * width, width), width)
        mine[c] = mm(act, wdown_ref[:, columns]).astype(BF16)
        if i < n_cuts - 1:
            copy = remote(mine.at[c], halves.at[cut], half_send.at[i], half_recv.at[cut], (dp, c))
            copy.start()
            sent.append(copy)
    summed = mine[cut].astype(F32)
    for i, c in enumerate(cut_peers):
        remote(mine.at[c], halves.at[c], half_send.at[i], half_recv.at[c], (dp, c)).wait_recv()
        summed = summed + halves[c].astype(F32)
    share[...] = summed.astype(BF16).reshape(GROUP, per_group, width)

    for j, h in enumerate(g_peers):
        copy = remote(share.at[h], red.at[g], red_send.at[j], red_recv.at[g], (me * GROUP + h, cut))
        copy.start()
        sent.append(copy)
    nq = min(TILE // slots, width // 128)
    piece = width // nq
    row, col = iota((n_e * TILE, nq * per_group), 0), iota((n_e * TILE, nq * per_group), 1)
    repack = one_hot(
        (div(mod(row, TILE), slots) == div(col, per_group))
        & (div(row, TILE) * slots + mod(row, slots) == mod(col, per_group))
    )
    summed = share[g].astype(F32)
    for j, h in enumerate(g_peers):
        remote(share.at[h], red.at[h], red_send.at[j], red_recv.at[h], (me * GROUP + h, cut)).wait_recv()
        summed = summed + red[h].astype(F32)
    stacked = jnp.concatenate([summed[:, k * piece : (k + 1) * piece] for k in range(nq)], axis=0)
    going[...] = mm(repack, stacked.astype(BF16)).astype(BF16).reshape(n_e, TILE, piece)

    for i, e in enumerate(e_peers):
        copy = remote(
            going.at[e], back.at[me], back_send.at[i], back_recv.at[me], (e * GROUP + g, cut)
        )
        copy.start()
        sent.append(copy)
    back[me] = going[me]
    table_shape = (count, n_e * TILE)
    row, col = iota(table_shape, 0), iota(table_shape, 1)
    target = jnp.zeros(table_shape, jnp.int32)
    for t in range(count):
        target = jnp.where(row == t, place[t], target)
    found = div(col, TILE) * slots + mod(col, slots) == target
    picks = [one_hot(found & (div(mod(col, TILE), slots) == k)) for k in range(nq)]
    for i, e in enumerate(e_peers):
        remote(
            going.at[e], back.at[e], back_send.at[i], back_recv.at[e], (e * GROUP + g, cut)
        ).wait_recv()
    returned = back[...].reshape(n_e * TILE, piece)
    expert_cols = jnp.concatenate([mm(pick, returned) for pick in picks], axis=1)
    hidden_cols = hid_ref[:, pl.ds(pl.multiple_of(cut * width, width), width)]
    out_ref[...] = (hidden_cols + expert_cols).astype(BF16)
    for copy in sent:
        copy.wait_send()


def on_device(
    n_data,
    n_cuts,
    queries,
    new_keys,
    new_values,
    key_cache,
    value_cache,
    lengths,
    resid,
    norm_gain,
    w_out,
    experts,
    w_up,
    w_down,
):
    count, feats = queries.shape
    width_all = resid.shape[1]
    width = width_all // n_cuts
    n_e = n_data // GROUP
    slots = max(2, 2 * count * GROUP // n_data)
    chunk = width_all * slots // TILE
    piece = width // min(TILE // slots, width // 128)
    per_group = n_e * slots
    all_rows = GROUP * per_group
    dma = pltpu.SemaphoreType.DMA
    smem = pl.BlockSpec(memory_space=pltpu.SMEM)
    hbm = pl.BlockSpec(memory_space=pl.ANY)
    return pl.pallas_call(
        functools.partial(kernel, n_data, n_cuts),
        out_shape=jax.ShapeDtypeStruct((count, width), BF16),
        in_specs=[smem, smem] + [hbm] * 10,
        out_specs=pl.BlockSpec(memory_space=pltpu.VMEM),
        scratch_shapes=[
            pltpu.VMEM(queries.shape, BF16),
            pltpu.VMEM(new_keys.shape, BF16),
            pltpu.VMEM(new_values.shape, BF16),
            pltpu.VMEM(key_cache.shape, BF16),
            pltpu.VMEM(value_cache.shape, BF16),
            pltpu.VMEM(resid.shape, BF16),
            pltpu.VMEM((1, width_all), F32),
            pltpu.VMEM(w_out.shape, BF16),
            pltpu.VMEM(w_up.shape[1:], BF16),
            pltpu.VMEM(w_down.shape[1:], BF16),
            pltpu.VMEM((n_cuts, count, width_all), F32),
            pltpu.VMEM((count, width_all), F32),
            pltpu.VMEM((n_e, TILE, chunk), BF16),
            pltpu.VMEM((GROUP, n_e, TILE, chunk), BF16),
            pltpu.VMEM((n_cuts, all_rows, width), BF16),
            pltpu.VMEM((n_cuts, all_rows, width), BF16),
            pltpu.VMEM((GROUP, per_group, width), BF16),
            pltpu.VMEM((GROUP, per_group, width), BF16),
            pltpu.VMEM((n_e, TILE, piece), BF16),
            pltpu.VMEM((n_e, TILE, piece), BF16),
            dma((10,)),
            dma((n_cuts,)),
            dma((n_cuts,)),
            dma((n_e,)),
            dma((n_e,)),
            dma((GROUP, n_e)),
            dma((GROUP, n_e)),
            dma((n_cuts,)),
            dma((n_cuts,)),
            dma((GROUP,)),
            dma((GROUP,)),
            dma((n_e,)),
            dma((n_e,)),
        ],
        compiler_params=pltpu.CompilerParams(
            collective_id=0, has_side_effects=True, vmem_limit_bytes=48 * 1024 * 1024
        ),
    )(
        lengths,
        experts.reshape(count),
        queries,
        new_keys,
        new_values,
        key_cache,
        value_cache,
        resid,
        norm_gain.reshape(1, width_all),
        w_out,
        w_up,
        w_down,
    )


def solution(mesh):
    placed = (
        P("dp", "cuts"),
        P("dp", "cuts"),
        P("dp", "cuts"),
        P("dp", None, "cuts"),
        P("dp", None, "cuts"),
        P("dp"),
        P("dp", None),
        P(),
        P("cuts", None),
        P("dp", None),
        P("dp", None, "cuts"),
        P("dp", "cuts", None),
    )
    return jax.shard_map(
        functools.partial(on_device, mesh.shape["dp"], mesh.shape["cuts"]),
        mesh=mesh,
        in_specs=placed,
        out_specs=P("dp", "cuts"),
        check_vma=False,
    )
```

```python
import functools

import jax
import jax.numpy as jnp
from jax import lax
from jax.experimental import pallas as pl
from jax.experimental.pallas import tpu as pltpu
from jax.sharding import PartitionSpec as P

HD = 128
GROUP = 4
TILE = 16
MESH = pl.DeviceIdType.MESH
F32 = jnp.float32
BF16 = jnp.bfloat16


def iota(shape, dim):
    return lax.broadcasted_iota(jnp.int32, shape, dim)


def div(x, n):
    return x >> (n.bit_length() - 1)


def mod(x, n):
    return x & (n - 1)


def one_hot(flags):
    return jnp.where(flags, 1.0, 0.0).astype(BF16)


def mm(a, b):
    return jnp.dot(a, b, preferred_element_type=F32)


def kernel(
    n_data,
    n_cuts,
    lengths_hbm,
    experts_hbm,
    q_hbm,
    nk_hbm,
    nv_hbm,
    k_hbm,
    v_hbm,
    resid_hbm,
    gain_hbm,
    wout_hbm,
    wup_hbm,
    wdown_hbm,
    out_ref,
    lengths,
    experts,
    q_ref,
    nk_ref,
    nv_ref,
    k_ref,
    v_ref,
    resid_ref,
    gain_ref,
    wout_ref,
    wup_ref,
    wdown_ref,
    parts,
    hid_ref,
    packed,
    gath,
    mine,
    halves,
    share,
    red,
    going,
    back,
    load_sem,
    part_send,
    part_recv,
    z_send,
    z_recv,
    spread_send,
    spread_recv,
    cross_send,
    cross_recv,
    half_send,
    half_recv,
    red_send,
    red_recv,
    back_send,
    back_recv,
):
    dp = lax.axis_index("dp")
    cut = lax.axis_index("cuts")
    me = dp // GROUP
    g = lax.rem(dp, GROUP)
    n_e = n_data // GROUP
    count, feats = q_ref.shape
    width_all = resid_ref.shape[1]
    width = width_all // n_cuts
    heads = feats // HD
    length = k_hbm.shape[1]
    slots = max(2, 2 * count * GROUP // n_data)
    scale = 1.0 / HD**0.5

    loads = [
        pltpu.make_async_copy(src, dst, load_sem.at[i])
        for i, (src, dst) in enumerate(
            (
                (q_hbm, q_ref),
                (nk_hbm, nk_ref),
                (k_hbm, k_ref),
                (nv_hbm, nv_ref),
                (v_hbm, v_ref),
                (resid_hbm, resid_ref),
                (gain_hbm, gain_ref),
                (wout_hbm, wout_ref),
                (wup_hbm.at[0], wup_ref),
                (wdown_hbm.at[0], wdown_ref),
                (lengths_hbm, lengths),
                (experts_hbm, experts),
            )
        )
    ]
    for i in (0, 2, 1, 10, 4, 3, 11, 5, 6):
        loads[i].start()

    cut_peers = [lax.rem(cut + d, n_cuts) for d in range(1, n_cuts)]
    e_peers = [lax.rem(me + d, n_e) for d in range(1, n_e)]
    g_peers = [lax.rem(g + d, GROUP) for d in range(1, GROUP)]
    ids = [(dp, c) for c in cut_peers]
    ids += [(e * GROUP + g, cut) for e in e_peers]
    ids += [(me * GROUP + h, cut) for h in g_peers]
    barrier = pltpu.get_barrier_semaphore()
    for device in ids:
        pl.semaphore_signal(barrier, inc=1, device_id=device, device_id_type=MESH)

    def remote(src, dst, send, recv, device):
        return pltpu.make_async_remote_copy(
            src_ref=src, dst_ref=dst, send_sem=send, recv_sem=recv, device_id=device, device_id_type=MESH
        )

    sent = []

    pairs = count * heads
    spread_rows = one_hot(div(iota((pairs, count), 0), heads) == iota((pairs, count), 1))
    own_head = div(iota((pairs, feats), 1), HD) == mod(iota((pairs, feats), 0), heads)
    loads[0].wait()
    q_wide = jnp.where(own_head, mm(spread_rows, q_ref[...]), 0.0).astype(BF16)
    nt = (((1,), (1,)), ((), ()))
    loads[1].wait()
    fresh_all = lax.dot_general(q_wide, nk_ref[...], nt, preferred_element_type=F32)
    own_new = div(iota((pairs, count), 0), heads) == iota((pairs, count), 1)
    fresh = jnp.sum(jnp.where(own_new, fresh_all, 0.0), axis=1, keepdims=True) * scale
    loads[2].wait()
    loads[7].start()
    loads[10].wait()
    span = count * length
    keys = k_ref[...].reshape(span, feats)
    scores = lax.dot_general(q_wide, keys, nt, preferred_element_type=F32) * scale
    col = iota((1, span), 1)
    limit = jnp.zeros((1, span), jnp.int32)
    for t in range(count):
        limit = jnp.where(div(col, length) == t, lengths[t], limit)
    valid = jnp.where(mod(col, length) < limit, div(col, length), -1)
    keep = div(iota((pairs, span), 0), heads) == valid
    scores = jnp.where(keep, scores, -1e30)
    peak = jnp.maximum(jnp.max(scores, axis=1, keepdims=True), fresh)
    pcache = jnp.where(keep, jnp.exp(scores - peak), 0.0)
    pnew = jnp.exp(fresh - peak)
    total = jnp.sum(pcache, axis=1, keepdims=True) + pnew
    pcache = (pcache / total).astype(BF16)
    pnew = (pnew / total).astype(BF16).astype(F32)
    loads[3].wait()
    new_rows = mm(spread_rows, nv_ref[...])
    loads[4].wait()
    loads[8].start()
    loads[9].start()
    summed = mm(pcache, v_ref[...].reshape(span, feats)) + pnew * new_rows
    summed = jnp.where(own_head, summed, 0.0).astype(BF16)
    join_rows = one_hot(div(iota((count, pairs), 1), heads) == iota((count, pairs), 0))
    heads_out = mm(join_rows, summed).astype(BF16)

    loads[7].wait()
    parts[cut] = mm(heads_out, wout_ref[...])
    pl.semaphore_wait(barrier, len(ids))
    for i, c in enumerate(cut_peers):
        copy = remote(parts.at[cut], parts.at[cut], part_send.at[i], part_recv.at[cut], (dp, c))
        copy.start()
        sent.append(copy)

    loads[11].wait()
    ids_of = [experts[t] for t in range(count)]
    place = []
    for t in range(count):
        slot = jnp.int32(0)
        for u in range(t):
            slot = slot + jnp.where(ids_of[u] == ids_of[t], 1, 0)
        place.append(ids_of[t] * slots + slot)
    nq = min(TILE // slots, width // 128)
    piece = width // nq
    table_shape = (n_e * TILE, nq * count)
    row, col = iota(table_shape, 0), iota(table_shape, 1)
    target = jnp.zeros(table_shape, jnp.int32)
    for t in range(count):
        target = jnp.where(mod(col, count) == t, place[t], target)
    pack = one_hot(
        (div(mod(row, TILE), slots) == div(col, count))
        & (div(row, TILE) * slots + mod(row, slots) == target)
    )
    loads[5].wait()
    loads[6].wait()
    for c in cut_peers:
        remote(parts.at[c], parts.at[c], part_send.at[0], part_recv.at[c], (dp, c)).wait_recv()
    attn = parts[0]
    for c in range(1, n_cuts):
        attn = attn + parts[c]
    hidden = resid_ref[...].astype(F32) + attn
    hid_ref[...] = hidden
    meansq = jnp.mean(hidden * hidden, axis=1, keepdims=True)
    own = pl.ds(pl.multiple_of(cut * width, width), width)
    normed = hid_ref[:, own] * lax.rsqrt(meansq + 1e-06) * gain_ref[:, own]
    stacked = jnp.concatenate([normed[:, k * piece : (k + 1) * piece] for k in range(nq)], axis=0)
    rows = mm(pack, stacked.astype(BF16)).astype(BF16)
    packed[...] = rows.reshape(n_e, TILE, piece)

    for i, e in enumerate(e_peers):
        copy = remote(
            packed.at[e], gath.at[cut, g, me], z_send.at[i], z_recv.at[me], (e * GROUP + g, cut)
        )
        copy.start()
        sent.append(copy)
    gath[cut, g, me] = packed[me]
    for i, e in enumerate([me] + e_peers):
        if i > 0:
            remote(
                packed.at[e], gath.at[cut, g, e], z_send.at[0], z_recv.at[e], (e * GROUP + g, cut)
            ).wait_recv()
        for j, h in enumerate(g_peers):
            copy = remote(
                gath.at[cut, g, e],
                gath.at[cut, g, e],
                spread_send.at[j, i],
                spread_recv.at[g, e],
                (me * GROUP + h, cut),
            )
            copy.start()
            sent.append(copy)
    all_rows = GROUP * n_e * slots
    per_group = n_e * slots
    wide = GROUP * n_e * TILE
    row, col = iota((nq * all_rows, wide), 0), iota((nq * all_rows, wide), 1)
    which, m = div(row, all_rows), mod(row, all_rows)
    unpack = one_hot(col == div(m, slots) * TILE + which * slots + mod(m, slots))
    for j, h in enumerate([g] + g_peers):
        if j > 0:
            for i, e in enumerate([me] + e_peers):
                remote(
                    gath.at[cut, h, e],
                    gath.at[cut, h, e],
                    spread_send.at[0, 0],
                    spread_recv.at[h, e],
                    (me * GROUP + h, cut),
                ).wait_recv()
        for i, c in enumerate(cut_peers):
            copy = remote(
                gath.at[cut, h], gath.at[cut, h], cross_send.at[i, j], cross_recv.at[cut, h], (dp, c)
            )
            copy.start()
            sent.append(copy)

    loads[8].wait()
    up = jnp.zeros((all_rows, wup_ref.shape[1]), F32)
    for i, c in enumerate([cut] + cut_peers):
        if i > 0:
            for h in range(GROUP):
                remote(
                    gath.at[c, h], gath.at[c, h], cross_send.at[0, 0], cross_recv.at[c, h], (dp, c)
                ).wait_recv()
        arrived = mm(unpack, gath[c].reshape(wide, piece)).astype(BF16)
        for k in range(nq):
            depth = pl.ds(pl.multiple_of(c * width + k * piece, piece), piece)
            up = up + mm(arrived[k * all_rows : (k + 1) * all_rows], wup_ref[depth, :])
    act = jax.nn.gelu(up).astype(BF16)

    loads[9].wait()
    for i, c in enumerate(cut_peers + [cut]):
        columns = pl.ds(pl.multiple_of(c * width, width), width)
        mine[c] = mm(act, wdown_ref[:, columns]).astype(BF16)
        if i < n_cuts - 1:
            copy = remote(mine.at[c], halves.at[cut], half_send.at[i], half_recv.at[cut], (dp, c))
            copy.start()
            sent.append(copy)
    summed = mine[cut].astype(F32)
    for i, c in enumerate(cut_peers):
        remote(mine.at[c], halves.at[c], half_send.at[i], half_recv.at[c], (dp, c)).wait_recv()
        summed = summed + halves[c].astype(F32)
    share[...] = summed.astype(BF16).reshape(GROUP, per_group, width)

    for j, h in enumerate(g_peers):
        copy = remote(share.at[h], red.at[g], red_send.at[j], red_recv.at[g], (me * GROUP + h, cut))
        copy.start()
        sent.append(copy)
    row, col = iota((n_e * TILE, nq * per_group), 0), iota((n_e * TILE, nq * per_group), 1)
    repack = one_hot(
        (div(mod(row, TILE), slots) == div(col, per_group))
        & (div(row, TILE) * slots + mod(row, slots) == mod(col, per_group))
    )
    summed = share[g].astype(F32)
    for j, h in enumerate(g_peers):
        remote(share.at[h], red.at[h], red_send.at[j], red_recv.at[h], (me * GROUP + h, cut)).wait_recv()
        summed = summed + red[h].astype(F32)
    stacked = jnp.concatenate([summed[:, k * piece : (k + 1) * piece] for k in range(nq)], axis=0)
    going[...] = mm(repack, stacked.astype(BF16)).astype(BF16).reshape(n_e, TILE, piece)

    for i, e in enumerate(e_peers):
        copy = remote(
            going.at[e], back.at[me], back_send.at[i], back_recv.at[me], (e * GROUP + g, cut)
        )
        copy.start()
        sent.append(copy)
    back[me] = going[me]
    table_shape = (count, n_e * TILE)
    row, col = iota(table_shape, 0), iota(table_shape, 1)
    target = jnp.zeros(table_shape, jnp.int32)
    for t in range(count):
        target = jnp.where(row == t, place[t], target)
    found = div(col, TILE) * slots + mod(col, slots) == target
    picks = [one_hot(found & (div(mod(col, TILE), slots) == k)) for k in range(nq)]
    for i, e in enumerate(e_peers):
        remote(
            going.at[e], back.at[e], back_send.at[i], back_recv.at[e], (e * GROUP + g, cut)
        ).wait_recv()
    returned = back[...].reshape(n_e * TILE, piece)
    expert_cols = jnp.concatenate([mm(pick, returned) for pick in picks], axis=1)
    out_ref[...] = (hid_ref[:, own] + expert_cols).astype(BF16)
    for copy in sent:
        copy.wait_send()


def on_device(
    n_data,
    n_cuts,
    queries,
    new_keys,
    new_values,
    key_cache,
    value_cache,
    lengths,
    resid,
    norm_gain,
    w_out,
    experts,
    w_up,
    w_down,
):
    count, feats = queries.shape
    width_all = resid.shape[1]
    width = width_all // n_cuts
    n_e = n_data // GROUP
    slots = max(2, 2 * count * GROUP // n_data)
    piece = width // min(TILE // slots, width // 128)
    per_group = n_e * slots
    all_rows = GROUP * per_group
    dma = pltpu.SemaphoreType.DMA
    hbm = pl.BlockSpec(memory_space=pltpu.HBM)
    return pl.pallas_call(
        functools.partial(kernel, n_data, n_cuts),
        out_shape=jax.ShapeDtypeStruct((count, width), BF16),
        in_specs=[hbm] * 12,
        out_specs=pl.BlockSpec(memory_space=pltpu.VMEM),
        scratch_shapes=[
            pltpu.SMEM((count,), jnp.int32),
            pltpu.SMEM((count,), jnp.int32),
            pltpu.VMEM(queries.shape, BF16),
            pltpu.VMEM(new_keys.shape, BF16),
            pltpu.VMEM(new_values.shape, BF16),
            pltpu.VMEM(key_cache.shape, BF16),
            pltpu.VMEM(value_cache.shape, BF16),
            pltpu.VMEM(resid.shape, BF16),
            pltpu.VMEM((1, width_all), F32),
            pltpu.VMEM(w_out.shape, BF16),
            pltpu.VMEM(w_up.shape[1:], BF16),
            pltpu.VMEM(w_down.shape[1:], BF16),
            pltpu.VMEM((n_cuts, count, width_all), F32),
            pltpu.VMEM((count, width_all), F32),
            pltpu.VMEM((n_e, TILE, piece), BF16),
            pltpu.VMEM((n_cuts, GROUP, n_e, TILE, piece), BF16),
            pltpu.VMEM((n_cuts, all_rows, width), BF16),
            pltpu.VMEM((n_cuts, all_rows, width), BF16),
            pltpu.VMEM((GROUP, per_group, width), BF16),
            pltpu.VMEM((GROUP, per_group, width), BF16),
            pltpu.VMEM((n_e, TILE, piece), BF16),
            pltpu.VMEM((n_e, TILE, piece), BF16),
            dma((12,)),
            dma((n_cuts,)),
            dma((n_cuts,)),
            dma((n_e,)),
            dma((n_e,)),
            dma((GROUP, n_e)),
            dma((GROUP, n_e)),
            dma((n_cuts, GROUP)),
            dma((n_cuts, GROUP)),
            dma((n_cuts,)),
            dma((n_cuts,)),
            dma((GROUP,)),
            dma((GROUP,)),
            dma((n_e,)),
            dma((n_e,)),
        ],
        compiler_params=pltpu.CompilerParams(
            collective_id=0, has_side_effects=True, vmem_limit_bytes=60 * 1024 * 1024
        ),
    )(
        lengths,
        experts.reshape(count),
        queries,
        new_keys,
        new_values,
        key_cache,
        value_cache,
        resid,
        norm_gain.reshape(1, width_all),
        w_out,
        w_up,
        w_down,
    )


def solution(mesh):
    placed = (
        P("dp", "cuts"),
        P("dp", "cuts"),
        P("dp", "cuts"),
        P("dp", None, "cuts"),
        P("dp", None, "cuts"),
        P("dp"),
        P("dp", None),
        P(),
        P("cuts", None),
        P("dp", None),
        P("dp", None, "cuts"),
        P("dp", "cuts", None),
    )
    return jax.shard_map(
        functools.partial(on_device, mesh.shape["dp"], mesh.shape["cuts"]),
        mesh=mesh,
        in_specs=placed,
        out_specs=P("dp", "cuts"),
        check_vma=False,
    )
```

```python
import functools

import jax
import jax.numpy as jnp
from jax import lax
from jax.experimental import pallas as pl
from jax.experimental.pallas import tpu as pltpu
from jax.sharding import PartitionSpec as P

HD = 128
GROUP = 4
TILE = 16
MESH = pl.DeviceIdType.MESH
F32 = jnp.float32
BF16 = jnp.bfloat16


def iota(shape, dim):
    return lax.broadcasted_iota(jnp.int32, shape, dim)


def div(x, n):
    return x >> (n.bit_length() - 1)


def mod(x, n):
    return x & (n - 1)


def one_hot(flags):
    return jnp.where(flags, 1.0, 0.0).astype(BF16)


def mm(a, b):
    return jnp.dot(a, b, preferred_element_type=F32)


def kernel(
    n_data,
    n_cuts,
    lengths_hbm,
    experts_hbm,
    q_hbm,
    nk_hbm,
    nv_hbm,
    k_hbm,
    v_hbm,
    resid_hbm,
    gain_hbm,
    wout_hbm,
    wup_hbm,
    wdown_hbm,
    out_ref,
    lengths,
    experts,
    q_ref,
    nk_ref,
    nv_ref,
    k_ref,
    v_ref,
    resid_ref,
    gain_ref,
    wout_ref,
    wup_ref,
    wdown_ref,
    parts,
    hid_ref,
    packed,
    gath,
    mine,
    halves,
    share,
    red,
    going,
    back,
    load_sem,
    part_send,
    part_recv,
    z_send,
    z_recv,
    spread_send,
    spread_recv,
    cross_send,
    cross_recv,
    half_send,
    half_recv,
    red_send,
    red_recv,
    back_send,
    back_recv,
):
    dp = lax.axis_index("dp")
    cut = lax.axis_index("cuts")
    me = dp // GROUP
    g = lax.rem(dp, GROUP)
    n_e = n_data // GROUP
    count, feats = q_ref.shape
    width_all = resid_ref.shape[1]
    width = width_all // n_cuts
    heads = feats // HD
    length = k_hbm.shape[1]
    slots = max(2, 2 * count * GROUP // n_data)
    scale = 1.0 / HD**0.5

    loads = [
        pltpu.make_async_copy(src, dst, load_sem.at[i])
        for i, (src, dst) in enumerate(
            (
                (q_hbm, q_ref),
                (nk_hbm, nk_ref),
                (k_hbm, k_ref),
                (nv_hbm, nv_ref),
                (v_hbm, v_ref),
                (resid_hbm, resid_ref),
                (gain_hbm, gain_ref),
                (wout_hbm, wout_ref),
                (wup_hbm.at[0], wup_ref),
                (wdown_hbm.at[0], wdown_ref),
                (lengths_hbm, lengths),
                (experts_hbm, experts),
            )
        )
    ]
    for i in (0, 10, 2, 1, 4, 3, 11, 5, 6):
        loads[i].start()

    cut_peers = [lax.rem(cut + d, n_cuts) for d in range(1, n_cuts)]
    e_peers = [lax.rem(me + d, n_e) for d in range(1, n_e)]
    g_peers = [lax.rem(g + d, GROUP) for d in range(1, GROUP)]
    ids = [(dp, c) for c in cut_peers]
    ids += [(e * GROUP + g, cut) for e in e_peers]
    ids += [(me * GROUP + h, cut) for h in g_peers]
    barrier = pltpu.get_barrier_semaphore()
    for device in ids:
        pl.semaphore_signal(barrier, inc=1, device_id=device, device_id_type=MESH)

    def remote(src, dst, send, recv, device):
        return pltpu.make_async_remote_copy(
            src_ref=src, dst_ref=dst, send_sem=send, recv_sem=recv, device_id=device, device_id_type=MESH
        )

    sent = []

    pairs = count * heads
    spread_rows = one_hot(div(iota((pairs, count), 0), heads) == iota((pairs, count), 1))
    own_head = div(iota((pairs, feats), 1), HD) == mod(iota((pairs, feats), 0), heads)
    loads[0].wait()
    q_wide = jnp.where(own_head, mm(spread_rows, q_ref[...]), 0.0).astype(BF16)
    nt = (((1,), (1,)), ((), ()))
    loads[1].wait()
    fresh_all = lax.dot_general(q_wide, nk_ref[...], nt, preferred_element_type=F32)
    own_new = div(iota((pairs, count), 0), heads) == iota((pairs, count), 1)
    fresh = jnp.sum(jnp.where(own_new, fresh_all, 0.0), axis=1, keepdims=True) * scale
    loads[10].wait()
    span = count * length
    col = iota((1, span), 1)
    limit = jnp.zeros((1, span), jnp.int32)
    for t in range(count):
        limit = jnp.where(div(col, length) == t, lengths[t], limit)
    valid = jnp.where(mod(col, length) < limit, div(col, length), -1)
    keep = div(iota((pairs, span), 0), heads) == valid
    loads[2].wait()
    loads[7].start()
    keys = k_ref[...].reshape(span, feats)
    scores = lax.dot_general(q_wide, keys, nt, preferred_element_type=F32) * scale
    scores = jnp.where(keep, scores, -1e30)
    peak = jnp.maximum(jnp.max(scores, axis=1, keepdims=True), fresh)
    pcache = jnp.where(keep, jnp.exp(scores - peak), 0.0)
    pnew = jnp.exp(fresh - peak)
    total = jnp.sum(pcache, axis=1, keepdims=True) + pnew
    pcache = (pcache / total).astype(BF16)
    pnew = (pnew / total).astype(BF16).astype(F32)
    loads[3].wait()
    new_rows = mm(spread_rows, nv_ref[...])
    loads[4].wait()
    loads[8].start()
    loads[9].start()
    summed = mm(pcache, v_ref[...].reshape(span, feats)) + pnew * new_rows
    summed = jnp.where(own_head, summed, 0.0).astype(BF16)
    join_rows = one_hot(div(iota((count, pairs), 1), heads) == iota((count, pairs), 0))
    heads_out = mm(join_rows, summed).astype(BF16)

    loads[7].wait()
    parts[cut] = mm(heads_out, wout_ref[...])
    pl.semaphore_wait(barrier, len(ids))
    for i, c in enumerate(cut_peers):
        copy = remote(parts.at[cut], parts.at[cut], part_send.at[i], part_recv.at[cut], (dp, c))
        copy.start()
        sent.append(copy)

    loads[11].wait()
    ids_of = [experts[t] for t in range(count)]
    place = []
    for t in range(count):
        slot = jnp.int32(0)
        for u in range(t):
            slot = slot + jnp.where(ids_of[u] == ids_of[t], 1, 0)
        place.append(ids_of[t] * slots + slot)
    nq = min(TILE // slots, width // 128)
    piece = width // nq
    table_shape = (n_e * TILE, nq * count)
    row, col = iota(table_shape, 0), iota(table_shape, 1)
    target = jnp.zeros(table_shape, jnp.int32)
    for t in range(count):
        target = jnp.where(mod(col, count) == t, place[t], target)
    pack = one_hot(
        (div(mod(row, TILE), slots) == div(col, count))
        & (div(row, TILE) * slots + mod(row, slots) == target)
    )
    loads[5].wait()
    loads[6].wait()
    for c in cut_peers:
        remote(parts.at[c], parts.at[c], part_send.at[0], part_recv.at[c], (dp, c)).wait_recv()
    attn = parts[0]
    for c in range(1, n_cuts):
        attn = attn + parts[c]
    hidden = resid_ref[...].astype(F32) + attn
    hid_ref[...] = hidden
    meansq = jnp.mean(hidden * hidden, axis=1, keepdims=True)
    own = pl.ds(pl.multiple_of(cut * width, width), width)
    normed = hid_ref[:, own] * lax.rsqrt(meansq + 1e-06) * gain_ref[:, own]
    stacked = jnp.concatenate([normed[:, k * piece : (k + 1) * piece] for k in range(nq)], axis=0)
    rows = mm(pack, stacked.astype(BF16)).astype(BF16)
    packed[...] = rows.reshape(n_e, TILE, piece)

    for i, e in enumerate(e_peers):
        copy = remote(
            packed.at[e], gath.at[cut, g, me], z_send.at[i], z_recv.at[me], (e * GROUP + g, cut)
        )
        copy.start()
        sent.append(copy)
    gath[cut, g, me] = packed[me]
    for e in e_peers:
        remote(
            packed.at[e], gath.at[cut, g, e], z_send.at[0], z_recv.at[e], (e * GROUP + g, cut)
        ).wait_recv()
    for j, h in enumerate(g_peers):
        copy = remote(
            gath.at[cut, g], gath.at[cut, g], spread_send.at[j], spread_recv.at[g], (me * GROUP + h, cut)
        )
        copy.start()
        sent.append(copy)
    all_rows = GROUP * n_e * slots
    per_group = n_e * slots
    wide = GROUP * n_e * TILE
    row, col = iota((nq * all_rows, wide), 0), iota((nq * all_rows, wide), 1)
    which, m = div(row, all_rows), mod(row, all_rows)
    unpack = one_hot(col == div(m, slots) * TILE + which * slots + mod(m, slots))
    for j, h in enumerate([g] + g_peers):
        if j > 0:
            remote(
                gath.at[cut, h], gath.at[cut, h], spread_send.at[0], spread_recv.at[h], (me * GROUP + h, cut)
            ).wait_recv()
        for i, c in enumerate(cut_peers):
            copy = remote(
                gath.at[cut, h], gath.at[cut, h], cross_send.at[i, j], cross_recv.at[cut, h], (dp, c)
            )
            copy.start()
            sent.append(copy)

    loads[8].wait()
    up = None
    for i, c in enumerate([cut] + cut_peers):
        if i > 0:
            for h in range(GROUP):
                remote(
                    gath.at[c, h], gath.at[c, h], cross_send.at[0, 0], cross_recv.at[c, h], (dp, c)
                ).wait_recv()
        arrived = mm(unpack, gath[c].reshape(wide, piece)).astype(BF16)
        arrived = jnp.concatenate(
            [arrived[k * all_rows : (k + 1) * all_rows] for k in range(nq)], axis=1
        )
        term = mm(arrived, wup_ref[pl.ds(pl.multiple_of(c * width, width), width), :])
        up = term if up is None else up + term
    act = jax.nn.gelu(up).astype(BF16)

    loads[9].wait()
    runs, run = share.shape[0], share.shape[3]

    def down(c, r):
        columns = pl.ds(pl.multiple_of(c * width + r * run, run), run)
        return mm(act, wdown_ref[:, columns]).astype(BF16)

    for i, c in enumerate(cut_peers):
        for r in range(runs):
            mine[c, r] = down(c, r)
            copy = remote(
                mine.at[c, r], halves.at[cut, r], half_send.at[i, r], half_recv.at[cut, r], (dp, c)
            )
            copy.start()
            sent.append(copy)
    for r in range(runs):
        summed = down(cut, r).astype(F32)
        for c in cut_peers:
            remote(
                mine.at[c, r], halves.at[c, r], half_send.at[0, r], half_recv.at[c, r], (dp, c)
            ).wait_recv()
            summed = summed + halves[c, r].astype(F32)
        share[r] = summed.astype(BF16).reshape(GROUP, per_group, run)
        for j, h in enumerate(g_peers):
            copy = remote(
                share.at[r, h], red.at[r, g], red_send.at[r, j], red_recv.at[r, g], (me * GROUP + h, cut)
            )
            copy.start()
            sent.append(copy)
    row, col = iota((n_e * TILE, nq * per_group), 0), iota((n_e * TILE, nq * per_group), 1)
    repack = one_hot(
        (div(mod(row, TILE), slots) == div(col, per_group))
        & (div(row, TILE) * slots + mod(row, slots) == mod(col, per_group))
    )
    totals = []
    for r in range(runs):
        summed = share[r, g].astype(F32)
        for h in g_peers:
            remote(
                share.at[r, h], red.at[r, h], red_send.at[r, 0], red_recv.at[r, h], (me * GROUP + h, cut)
            ).wait_recv()
            summed = summed + red[r, h].astype(F32)
        totals.append(summed)
    summed = jnp.concatenate(totals, axis=1)
    stacked = jnp.concatenate([summed[:, k * piece : (k + 1) * piece] for k in range(nq)], axis=0)
    going[...] = mm(repack, stacked.astype(BF16)).astype(BF16).reshape(n_e, TILE, piece)

    for i, e in enumerate(e_peers):
        copy = remote(
            going.at[e], back.at[me], back_send.at[i], back_recv.at[me], (e * GROUP + g, cut)
        )
        copy.start()
        sent.append(copy)
    back[me] = going[me]
    table_shape = (count, n_e * TILE)
    row, col = iota(table_shape, 0), iota(table_shape, 1)
    target = jnp.zeros(table_shape, jnp.int32)
    for t in range(count):
        target = jnp.where(row == t, place[t], target)
    found = div(col, TILE) * slots + mod(col, slots) == target
    picks = [one_hot(found & (div(mod(col, TILE), slots) == k)) for k in range(nq)]
    for copy in sent:
        copy.wait_send()
    for i, e in enumerate(e_peers):
        remote(
            going.at[e], back.at[e], back_send.at[i], back_recv.at[e], (e * GROUP + g, cut)
        ).wait_recv()
    returned = back[...].reshape(n_e * TILE, piece)
    expert_cols = jnp.concatenate([mm(pick, returned) for pick in picks], axis=1)
    out_ref[...] = (hid_ref[:, own] + expert_cols).astype(BF16)


def on_device(
    n_data,
    n_cuts,
    queries,
    new_keys,
    new_values,
    key_cache,
    value_cache,
    lengths,
    resid,
    norm_gain,
    w_out,
    experts,
    w_up,
    w_down,
):
    count, feats = queries.shape
    width_all = resid.shape[1]
    width = width_all // n_cuts
    n_e = n_data // GROUP
    slots = max(2, 2 * count * GROUP // n_data)
    piece = width // min(TILE // slots, width // 128)
    per_group = n_e * slots
    all_rows = GROUP * per_group
    runs = 2 if width % 256 == 0 else 1
    run = width // runs
    dma = pltpu.SemaphoreType.DMA
    hbm = pl.BlockSpec(memory_space=pltpu.HBM)
    return pl.pallas_call(
        functools.partial(kernel, n_data, n_cuts),
        out_shape=pltpu.VMEM((count, width), BF16),
        in_specs=[hbm] * 12,
        out_specs=pl.BlockSpec(memory_space=pltpu.VMEM),
        scratch_shapes=[
            pltpu.SMEM((count,), jnp.int32),
            pltpu.SMEM((count,), jnp.int32),
            pltpu.VMEM(queries.shape, BF16),
            pltpu.VMEM(new_keys.shape, BF16),
            pltpu.VMEM(new_values.shape, BF16),
            pltpu.VMEM(key_cache.shape, BF16),
            pltpu.VMEM(value_cache.shape, BF16),
            pltpu.VMEM(resid.shape, BF16),
            pltpu.VMEM((1, width_all), F32),
            pltpu.VMEM(w_out.shape, BF16),
            pltpu.VMEM(w_up.shape[1:], BF16),
            pltpu.VMEM(w_down.shape[1:], BF16),
            pltpu.VMEM((n_cuts, count, width_all), F32),
            pltpu.VMEM((count, width_all), F32),
            pltpu.VMEM((n_e, TILE, piece), BF16),
            pltpu.VMEM((n_cuts, GROUP, n_e, TILE, piece), BF16),
            pltpu.VMEM((n_cuts, runs, all_rows, run), BF16),
            pltpu.VMEM((n_cuts, runs, all_rows, run), BF16),
            pltpu.VMEM((runs, GROUP, per_group, run), BF16),
            pltpu.VMEM((runs, GROUP, per_group, run), BF16),
            pltpu.VMEM((n_e, TILE, piece), BF16),
            pltpu.VMEM((n_e, TILE, piece), BF16),
            dma((12,)),
            dma((n_cuts,)),
            dma((n_cuts,)),
            dma((n_e,)),
            dma((n_e,)),
            dma((GROUP,)),
            dma((GROUP,)),
            dma((n_cuts, GROUP)),
            dma((n_cuts, GROUP)),
            dma((n_cuts, runs)),
            dma((n_cuts, runs)),
            dma((runs, GROUP)),
            dma((runs, GROUP)),
            dma((n_e,)),
            dma((n_e,)),
        ],
        compiler_params=pltpu.CompilerParams(
            collective_id=0, has_side_effects=True, vmem_limit_bytes=60 * 1024 * 1024
        ),
    )(
        lengths,
        experts.reshape(count),
        queries,
        new_keys,
        new_values,
        key_cache,
        value_cache,
        resid,
        norm_gain.reshape(1, width_all),
        w_out,
        w_up,
        w_down,
    )


def solution(mesh):
    placed = (
        P("dp", "cuts"),
        P("dp", "cuts"),
        P("dp", "cuts"),
        P("dp", None, "cuts"),
        P("dp", None, "cuts"),
        P("dp"),
        P("dp", None),
        P(),
        P("cuts", None),
        P("dp", None),
        P("dp", None, "cuts"),
        P("dp", "cuts", None),
    )
    return jax.shard_map(
        functools.partial(on_device, mesh.shape["dp"], mesh.shape["cuts"]),
        mesh=mesh,
        in_specs=placed,
        out_specs=P("dp", "cuts"),
        check_vma=False,
    )
```

```python
import functools

import jax
import jax.numpy as jnp
from jax import lax
from jax.experimental import pallas as pl
from jax.experimental.pallas import tpu as pltpu
from jax.sharding import PartitionSpec as P

HD = 128
GROUP = 4
TILE = 16
MESH = pl.DeviceIdType.MESH
F32 = jnp.float32
BF16 = jnp.bfloat16


def iota(shape, dim):
    return lax.broadcasted_iota(jnp.int32, shape, dim)


def div(x, n):
    return x >> (n.bit_length() - 1)


def mod(x, n):
    return x & (n - 1)


def one_hot(flags):
    return jnp.where(flags, 1.0, 0.0).astype(BF16)


def mm(a, b):
    return jnp.dot(a, b, preferred_element_type=F32)


def kernel(
    n_data,
    n_cuts,
    lengths_hbm,
    experts_hbm,
    q_hbm,
    nk_hbm,
    nv_hbm,
    k_hbm,
    v_hbm,
    resid_hbm,
    gain_hbm,
    wout_hbm,
    wup_hbm,
    wdown_hbm,
    out_ref,
    lengths,
    experts,
    q_ref,
    nk_ref,
    nv_ref,
    k_ref,
    v_ref,
    resid_ref,
    gain_ref,
    wout_ref,
    wup_ref,
    wdown_ref,
    parts,
    hid_ref,
    packed,
    gath,
    mine,
    halves,
    share,
    red,
    going,
    back,
    load_sem,
    part_send,
    part_recv,
    z_send,
    z_recv,
    spread_send,
    spread_recv,
    cross_send,
    cross_recv,
    half_send,
    half_recv,
    red_send,
    red_recv,
    back_send,
    back_recv,
):
    dp = lax.axis_index("dp")
    cut = lax.axis_index("cuts")
    me = dp // GROUP
    g = lax.rem(dp, GROUP)
    n_e = n_data // GROUP
    count, feats = q_ref.shape
    width_all = resid_ref.shape[1]
    width = width_all // n_cuts
    heads = feats // HD
    length = k_hbm.shape[1]
    slots = max(2, 2 * count * GROUP // n_data)
    scale = 1.0 / HD**0.5

    def pieces(src, dst, n, first):
        size = dst.shape[0] // n
        return [
            pltpu.make_async_copy(
                src.at[pl.ds(i * size, size)], dst.at[pl.ds(i * size, size)], load_sem.at[first + i]
            )
            for i in range(n)
        ]

    n_out = min(4, feats // 128)
    loads = [
        pltpu.make_async_copy(src, dst, load_sem.at[i])
        for i, (src, dst) in enumerate(
            (
                (q_hbm, q_ref),
                (lengths_hbm, lengths),
                (nk_hbm, nk_ref),
                (nv_hbm, nv_ref),
                (experts_hbm, experts),
                (resid_hbm, resid_ref),
                (gain_hbm, gain_ref),
            )
        )
    ]
    load_keys = pieces(k_hbm, k_ref, 2, 7)
    load_values = pieces(v_hbm, v_ref, 2, 9)
    load_out = pieces(wout_hbm, wout_ref, n_out, 11)
    load_up = pieces(wup_hbm.at[0], wup_ref, 4, 15)
    load_down = pieces(wdown_hbm.at[0], wdown_ref, 4, 19)
    for load in loads[:2] + load_keys + loads[2:3] + load_values + loads[3:]:
        load.start()

    cut_peers = [lax.rem(cut + d, n_cuts) for d in range(1, n_cuts)]
    e_peers = [lax.rem(me + d, n_e) for d in range(1, n_e)]
    g_peers = [lax.rem(g + d, GROUP) for d in range(1, GROUP)]
    ids = [(dp, c) for c in cut_peers]
    ids += [(e * GROUP + g, cut) for e in e_peers]
    ids += [(me * GROUP + h, cut) for h in g_peers]
    barrier = pltpu.get_barrier_semaphore()
    for device in ids:
        pl.semaphore_signal(barrier, inc=1, device_id=device, device_id_type=MESH)

    def remote(src, dst, send, recv, device):
        return pltpu.make_async_remote_copy(
            src_ref=src, dst_ref=dst, send_sem=send, recv_sem=recv, device_id=device, device_id_type=MESH
        )

    sent = []

    pairs = count * heads
    spread_rows = one_hot(div(iota((pairs, count), 0), heads) == iota((pairs, count), 1))
    own_head = div(iota((pairs, feats), 1), HD) == mod(iota((pairs, feats), 0), heads)
    loads[0].wait()
    for load in load_out:
        load.start()
    q_wide = jnp.where(own_head, mm(spread_rows, q_ref[...]), 0.0).astype(BF16)
    nt = (((1,), (1,)), ((), ()))
    loads[2].wait()
    fresh_all = lax.dot_general(q_wide, nk_ref[...], nt, preferred_element_type=F32)
    own_new = div(iota((pairs, count), 0), heads) == iota((pairs, count), 1)
    fresh = jnp.sum(jnp.where(own_new, fresh_all, 0.0), axis=1, keepdims=True) * scale
    loads[1].wait()
    span = count * length
    col = iota((1, span), 1)
    limit = jnp.zeros((1, span), jnp.int32)
    for t in range(count):
        limit = jnp.where(div(col, length) == t, lengths[t], limit)
    valid = jnp.where(mod(col, length) < limit, div(col, length), -1)
    keep = div(iota((pairs, span), 0), heads) == valid
    for load in load_keys:
        load.wait()
    keys = k_ref[...].reshape(span, feats)
    scores = lax.dot_general(q_wide, keys, nt, preferred_element_type=F32) * scale
    scores = jnp.where(keep, scores, -1e30)
    peak = jnp.maximum(jnp.max(scores, axis=1, keepdims=True), fresh)
    pcache = jnp.where(keep, jnp.exp(scores - peak), 0.0)
    pnew = jnp.exp(fresh - peak)
    total = jnp.sum(pcache, axis=1, keepdims=True) + pnew
    pcache = (pcache / total).astype(BF16)
    pnew = (pnew / total).astype(BF16).astype(F32)
    loads[3].wait()
    new_rows = mm(spread_rows, nv_ref[...])
    for load in load_values:
        load.wait()
    summed = mm(pcache, v_ref[...].reshape(span, feats)) + pnew * new_rows
    summed = jnp.where(own_head, summed, 0.0).astype(BF16)
    join_rows = one_hot(div(iota((count, pairs), 1), heads) == iota((count, pairs), 0))
    heads_out = mm(join_rows, summed).astype(BF16)

    depth = feats // n_out
    partial = jnp.zeros((count, width_all), F32)
    for i, load in enumerate(load_out):
        load.wait()
        if i == n_out - 1:
            for later in load_up + load_down:
                later.start()
        block = slice(i * depth, (i + 1) * depth)
        partial = partial + mm(heads_out[:, block], wout_ref[block, :])
    parts[cut] = partial
    pl.semaphore_wait(barrier, len(ids))
    for i, c in enumerate(cut_peers):
        copy = remote(parts.at[cut], parts.at[cut], part_send.at[i], part_recv.at[cut], (dp, c))
        copy.start()
        sent.append(copy)

    loads[4].wait()
    ids_of = [experts[t] for t in range(count)]
    place = []
    for t in range(count):
        slot = jnp.int32(0)
        for u in range(t):
            slot = slot + jnp.where(ids_of[u] == ids_of[t], 1, 0)
        place.append(ids_of[t] * slots + slot)
    nq = min(TILE // slots, width // 128)
    piece = width // nq
    table_shape = (n_e * TILE, nq * count)
    row, col = iota(table_shape, 0), iota(table_shape, 1)
    target = jnp.zeros(table_shape, jnp.int32)
    for t in range(count):
        target = jnp.where(mod(col, count) == t, place[t], target)
    pack = one_hot(
        (div(mod(row, TILE), slots) == div(col, count))
        & (div(row, TILE) * slots + mod(row, slots) == target)
    )
    loads[5].wait()
    loads[6].wait()
    for c in cut_peers:
        remote(parts.at[c], parts.at[c], part_send.at[0], part_recv.at[c], (dp, c)).wait_recv()
    attn = parts[0]
    for c in range(1, n_cuts):
        attn = attn + parts[c]
    hidden = resid_ref[...].astype(F32) + attn
    hid_ref[...] = hidden
    meansq = jnp.mean(hidden * hidden, axis=1, keepdims=True)
    own = pl.ds(pl.multiple_of(cut * width, width), width)
    normed = hid_ref[:, own] * lax.rsqrt(meansq + 1e-06) * gain_ref[:, own]
    stacked = jnp.concatenate([normed[:, k * piece : (k + 1) * piece] for k in range(nq)], axis=0)
    rows = mm(pack, stacked.astype(BF16)).astype(BF16)
    packed[...] = rows.reshape(n_e, TILE, piece)

    for i, e in enumerate(e_peers):
        copy = remote(
            packed.at[e], gath.at[cut, g, me], z_send.at[i], z_recv.at[me], (e * GROUP + g, cut)
        )
        copy.start()
        sent.append(copy)
    gath[cut, g, me] = packed[me]
    for e in e_peers:
        remote(
            packed.at[e], gath.at[cut, g, e], z_send.at[0], z_recv.at[e], (e * GROUP + g, cut)
        ).wait_recv()
    for j, h in enumerate(g_peers):
        copy = remote(
            gath.at[cut, g], gath.at[cut, g], spread_send.at[j], spread_recv.at[g], (me * GROUP + h, cut)
        )
        copy.start()
        sent.append(copy)
    all_rows = GROUP * n_e * slots
    per_group = n_e * slots
    wide = GROUP * n_e * TILE
    row, col = iota((nq * all_rows, wide), 0), iota((nq * all_rows, wide), 1)
    which, m = div(row, all_rows), mod(row, all_rows)
    unpack = one_hot(col == div(m, slots) * TILE + which * slots + mod(m, slots))
    for j, h in enumerate([g] + g_peers):
        if j > 0:
            remote(
                gath.at[cut, h], gath.at[cut, h], spread_send.at[0], spread_recv.at[h], (me * GROUP + h, cut)
            ).wait_recv()
        for i, c in enumerate(cut_peers):
            copy = remote(
                gath.at[cut, h], gath.at[cut, h], cross_send.at[i, j], cross_recv.at[cut, h], (dp, c)
            )
            copy.start()
            sent.append(copy)

    for load in load_up:
        load.wait()
    up = None
    for i, c in enumerate([cut] + cut_peers):
        if i > 0:
            for h in range(GROUP):
                remote(
                    gath.at[c, h], gath.at[c, h], cross_send.at[0, 0], cross_recv.at[c, h], (dp, c)
                ).wait_recv()
        arrived = mm(unpack, gath[c].reshape(wide, piece)).astype(BF16)
        arrived = jnp.concatenate(
            [arrived[k * all_rows : (k + 1) * all_rows] for k in range(nq)], axis=1
        )
        term = mm(arrived, wup_ref[pl.ds(pl.multiple_of(c * width, width), width), :])
        up = term if up is None else up + term
    act = jax.nn.gelu(up).astype(BF16)

    for load in load_down:
        load.wait()
    runs, run = share.shape[0], share.shape[3]

    def down(c, r):
        columns = pl.ds(pl.multiple_of(c * width + r * run, run), run)
        return mm(act, wdown_ref[:, columns]).astype(BF16)

    for i, c in enumerate(cut_peers):
        for r in range(runs):
            mine[c, r] = down(c, r)
            copy = remote(
                mine.at[c, r], halves.at[cut, r], half_send.at[i, r], half_recv.at[cut, r], (dp, c)
            )
            copy.start()
            sent.append(copy)
    for r in range(runs):
        summed = down(cut, r).astype(F32)
        for c in cut_peers:
            remote(
                mine.at[c, r], halves.at[c, r], half_send.at[0, r], half_recv.at[c, r], (dp, c)
            ).wait_recv()
            summed = summed + halves[c, r].astype(F32)
        share[r] = summed.astype(BF16).reshape(GROUP, per_group, run)
        for j, h in enumerate(g_peers):
            copy = remote(
                share.at[r, h], red.at[r, g], red_send.at[r, j], red_recv.at[r, g], (me * GROUP + h, cut)
            )
            copy.start()
            sent.append(copy)
    row, col = iota((n_e * TILE, nq * per_group), 0), iota((n_e * TILE, nq * per_group), 1)
    repack = one_hot(
        (div(mod(row, TILE), slots) == div(col, per_group))
        & (div(row, TILE) * slots + mod(row, slots) == mod(col, per_group))
    )
    totals = []
    for r in range(runs):
        summed = share[r, g].astype(F32)
        for h in g_peers:
            remote(
                share.at[r, h], red.at[r, h], red_send.at[r, 0], red_recv.at[r, h], (me * GROUP + h, cut)
            ).wait_recv()
            summed = summed + red[r, h].astype(F32)
        totals.append(summed)
    summed = jnp.concatenate(totals, axis=1)
    stacked = jnp.concatenate([summed[:, k * piece : (k + 1) * piece] for k in range(nq)], axis=0)
    going[...] = mm(repack, stacked.astype(BF16)).astype(BF16).reshape(n_e, TILE, piece)

    for i, e in enumerate(e_peers):
        copy = remote(
            going.at[e], back.at[me], back_send.at[i], back_recv.at[me], (e * GROUP + g, cut)
        )
        copy.start()
        sent.append(copy)
    back[me] = going[me]
    table_shape = (count, n_e * TILE)
    row, col = iota(table_shape, 0), iota(table_shape, 1)
    target = jnp.zeros(table_shape, jnp.int32)
    for t in range(count):
        target = jnp.where(row == t, place[t], target)
    found = div(col, TILE) * slots + mod(col, slots) == target
    picks = [one_hot(found & (div(mod(col, TILE), slots) == k)) for k in range(nq)]
    for copy in sent:
        copy.wait_send()
    for i, e in enumerate(e_peers):
        remote(
            going.at[e], back.at[e], back_send.at[i], back_recv.at[e], (e * GROUP + g, cut)
        ).wait_recv()
    returned = back[...].reshape(n_e * TILE, piece)
    expert_cols = jnp.concatenate([mm(pick, returned) for pick in picks], axis=1)
    out_ref[...] = (hid_ref[:, own] + expert_cols).astype(BF16)


def on_device(
    n_data,
    n_cuts,
    queries,
    new_keys,
    new_values,
    key_cache,
    value_cache,
    lengths,
    resid,
    norm_gain,
    w_out,
    experts,
    w_up,
    w_down,
):
    count, feats = queries.shape
    width_all = resid.shape[1]
    width = width_all // n_cuts
    n_e = n_data // GROUP
    slots = max(2, 2 * count * GROUP // n_data)
    piece = width // min(TILE // slots, width // 128)
    per_group = n_e * slots
    all_rows = GROUP * per_group
    runs = 2 if width % 256 == 0 else 1
    run = width // runs
    dma = pltpu.SemaphoreType.DMA
    hbm = pl.BlockSpec(memory_space=pltpu.HBM)
    return pl.pallas_call(
        functools.partial(kernel, n_data, n_cuts),
        out_shape=pltpu.VMEM((count, width), BF16),
        in_specs=[hbm] * 12,
        out_specs=pl.BlockSpec(memory_space=pltpu.VMEM),
        scratch_shapes=[
            pltpu.SMEM((count,), jnp.int32),
            pltpu.SMEM((count,), jnp.int32),
            pltpu.VMEM(queries.shape, BF16),
            pltpu.VMEM(new_keys.shape, BF16),
            pltpu.VMEM(new_values.shape, BF16),
            pltpu.VMEM(key_cache.shape, BF16),
            pltpu.VMEM(value_cache.shape, BF16),
            pltpu.VMEM(resid.shape, BF16),
            pltpu.VMEM((1, width_all), F32),
            pltpu.VMEM(w_out.shape, BF16),
            pltpu.VMEM(w_up.shape[1:], BF16),
            pltpu.VMEM(w_down.shape[1:], BF16),
            pltpu.VMEM((n_cuts, count, width_all), F32),
            pltpu.VMEM((count, width_all), F32),
            pltpu.VMEM((n_e, TILE, piece), BF16),
            pltpu.VMEM((n_cuts, GROUP, n_e, TILE, piece), BF16),
            pltpu.VMEM((n_cuts, runs, all_rows, run), BF16),
            pltpu.VMEM((n_cuts, runs, all_rows, run), BF16),
            pltpu.VMEM((runs, GROUP, per_group, run), BF16),
            pltpu.VMEM((runs, GROUP, per_group, run), BF16),
            pltpu.VMEM((n_e, TILE, piece), BF16),
            pltpu.VMEM((n_e, TILE, piece), BF16),
            dma((23,)),
            dma((n_cuts,)),
            dma((n_cuts,)),
            dma((n_e,)),
            dma((n_e,)),
            dma((GROUP,)),
            dma((GROUP,)),
            dma((n_cuts, GROUP)),
            dma((n_cuts, GROUP)),
            dma((n_cuts, runs)),
            dma((n_cuts, runs)),
            dma((runs, GROUP)),
            dma((runs, GROUP)),
            dma((n_e,)),
            dma((n_e,)),
        ],
        compiler_params=pltpu.CompilerParams(
            collective_id=0, has_side_effects=True, vmem_limit_bytes=60 * 1024 * 1024
        ),
    )(
        lengths,
        experts.reshape(count),
        queries,
        new_keys,
        new_values,
        key_cache,
        value_cache,
        resid,
        norm_gain.reshape(1, width_all),
        w_out,
        w_up,
        w_down,
    )


def solution(mesh):
    placed = (
        P("dp", "cuts"),
        P("dp", "cuts"),
        P("dp", "cuts"),
        P("dp", None, "cuts"),
        P("dp", None, "cuts"),
        P("dp"),
        P("dp", None),
        P(),
        P("cuts", None),
        P("dp", None),
        P("dp", None, "cuts"),
        P("dp", "cuts", None),
    )
    return jax.shard_map(
        functools.partial(on_device, mesh.shape["dp"], mesh.shape["cuts"]),
        mesh=mesh,
        in_specs=placed,
        out_specs=P("dp", "cuts"),
        check_vma=False,
    )
```

```python
import functools

import jax
import jax.numpy as jnp
from jax import lax
from jax.experimental import pallas as pl
from jax.experimental.pallas import tpu as pltpu
from jax.sharding import PartitionSpec as P

HD = 128
GROUP = 4
TILE = 16
MESH = pl.DeviceIdType.MESH
F32 = jnp.float32
BF16 = jnp.bfloat16


def iota(shape, dim):
    return lax.broadcasted_iota(jnp.int32, shape, dim)


def div(x, n):
    return x >> (n.bit_length() - 1)


def mod(x, n):
    return x & (n - 1)


def one_hot(flags):
    return jnp.where(flags, 1.0, 0.0).astype(BF16)


def mm(a, b):
    return jnp.dot(a, b, preferred_element_type=F32)


def kernel(
    n_data,
    n_cuts,
    lengths_hbm,
    experts_hbm,
    q_hbm,
    nk_hbm,
    nv_hbm,
    k_hbm,
    v_hbm,
    resid_hbm,
    gain_hbm,
    wout_hbm,
    wup_hbm,
    wdown_hbm,
    out_ref,
    lengths,
    experts,
    q_ref,
    nk_ref,
    nv_ref,
    k_ref,
    v_ref,
    resid_ref,
    gain_ref,
    wout_ref,
    wup_ref,
    wdown_ref,
    parts,
    hid_ref,
    packed,
    gath,
    mine,
    halves,
    share,
    red,
    going,
    back,
    load_sem,
    part_send,
    part_recv,
    z_send,
    z_recv,
    spread_send,
    spread_recv,
    cross_send,
    cross_recv,
    half_send,
    half_recv,
    red_send,
    red_recv,
    back_send,
    back_recv,
):
    dp = lax.axis_index("dp")
    cut = lax.axis_index("cuts")
    me = dp // GROUP
    g = lax.rem(dp, GROUP)
    n_e = n_data // GROUP
    count, feats = q_ref.shape
    width_all = resid_ref.shape[1]
    width = width_all // n_cuts
    heads = feats // HD
    length = k_hbm.shape[1]
    slots = max(2, 2 * count * GROUP // n_data)
    scale = 1.0 / HD**0.5

    def pieces(src, dst, n, first):
        size = dst.shape[0] // n
        return [
            pltpu.make_async_copy(
                src.at[pl.ds(i * size, size)], dst.at[pl.ds(i * size, size)], load_sem.at[first + i]
            )
            for i in range(n)
        ]

    n_out = min(4, feats // 128)
    loads = [
        pltpu.make_async_copy(src, dst, load_sem.at[i])
        for i, (src, dst) in enumerate(
            (
                (q_hbm, q_ref),
                (lengths_hbm, lengths),
                (nk_hbm, nk_ref),
                (nv_hbm, nv_ref),
                (experts_hbm, experts),
                (resid_hbm, resid_ref),
                (gain_hbm, gain_ref),
            )
        )
    ]
    load_keys = pieces(k_hbm, k_ref, 2, 7)
    load_values = pieces(v_hbm, v_ref, 2, 9)
    load_out = pieces(wout_hbm, wout_ref, n_out, 11)
    load_up = pieces(wup_hbm.at[0], wup_ref, 4, 15)
    load_down = pieces(wdown_hbm.at[0], wdown_ref, 4, 19)
    for load in loads[:2] + load_keys + loads[2:3] + load_values + loads[3:]:
        load.start()

    cut_peers = [lax.rem(cut + d, n_cuts) for d in range(1, n_cuts)]
    e_peers = [lax.rem(me + d, n_e) for d in range(1, n_e)]
    g_peers = [lax.rem(g + d, GROUP) for d in range(1, GROUP)]
    ids = [(dp, c) for c in cut_peers]
    ids += [(e * GROUP + g, cut) for e in e_peers]
    ids += [(me * GROUP + h, cut) for h in g_peers]
    barrier = pltpu.get_barrier_semaphore()
    for device in ids:
        pl.semaphore_signal(barrier, inc=1, device_id=device, device_id_type=MESH)

    def remote(src, dst, send, recv, device):
        return pltpu.make_async_remote_copy(
            src_ref=src, dst_ref=dst, send_sem=send, recv_sem=recv, device_id=device, device_id_type=MESH
        )

    sent = []

    pairs = count * heads
    spread_rows = one_hot(div(iota((pairs, count), 0), heads) == iota((pairs, count), 1))
    own_head = div(iota((pairs, feats), 1), HD) == mod(iota((pairs, feats), 0), heads)
    loads[0].wait()
    for load in load_out:
        load.start()
    q_wide = jnp.where(own_head, mm(spread_rows, q_ref[...]), 0.0).astype(BF16)
    nt = (((1,), (1,)), ((), ()))
    loads[2].wait()
    fresh_all = lax.dot_general(q_wide, nk_ref[...], nt, preferred_element_type=F32)
    own_new = div(iota((pairs, count), 0), heads) == iota((pairs, count), 1)
    fresh = jnp.sum(jnp.where(own_new, fresh_all, 0.0), axis=1, keepdims=True) * scale
    loads[1].wait()
    span = count * length
    col = iota((1, span), 1)
    limit = jnp.zeros((1, span), jnp.int32)
    for t in range(count):
        limit = jnp.where(div(col, length) == t, lengths[t], limit)
    valid = jnp.where(mod(col, length) < limit, div(col, length), -1)
    keep = div(iota((pairs, span), 0), heads) == valid
    for load in load_keys:
        load.wait()
    keys = k_ref[...].reshape(span, feats)
    scores = lax.dot_general(q_wide, keys, nt, preferred_element_type=F32) * scale
    scores = jnp.where(keep, scores, -1e30)
    peak = jnp.maximum(jnp.max(scores, axis=1, keepdims=True), fresh)
    pcache = jnp.where(keep, jnp.exp(scores - peak), 0.0)
    pnew = jnp.exp(fresh - peak)
    total = jnp.sum(pcache, axis=1, keepdims=True) + pnew
    pcache = (pcache / total).astype(BF16)
    pnew = (pnew / total).astype(BF16).astype(F32)
    loads[3].wait()
    new_rows = mm(spread_rows, nv_ref[...])
    for load in load_values:
        load.wait()
    summed = mm(pcache, v_ref[...].reshape(span, feats)) + pnew * new_rows
    summed = jnp.where(own_head, summed, 0.0).astype(BF16)
    join_rows = one_hot(div(iota((count, pairs), 1), heads) == iota((count, pairs), 0))
    heads_out = mm(join_rows, summed).astype(BF16)

    depth = feats // n_out
    partial = jnp.zeros((count, width_all), F32)
    for i, load in enumerate(load_out):
        load.wait()
        if i == n_out - 1:
            for later in load_up + load_down:
                later.start()
        block = slice(i * depth, (i + 1) * depth)
        partial = partial + mm(heads_out[:, block], wout_ref[block, :])
    parts[cut] = partial
    pl.semaphore_wait(barrier, len(ids))
    for i, c in enumerate(cut_peers):
        copy = remote(parts.at[cut], parts.at[cut], part_send.at[i], part_recv.at[cut], (dp, c))
        copy.start()
        sent.append(copy)

    loads[4].wait()
    ids_of = [experts[t] for t in range(count)]
    place = []
    for t in range(count):
        slot = jnp.int32(0)
        for u in range(t):
            slot = slot + jnp.where(ids_of[u] == ids_of[t], 1, 0)
        place.append(ids_of[t] * slots + slot)
    nq = min(TILE // slots, width // 128)
    piece = width // nq
    table_shape = (n_e * TILE, nq * count)
    row, col = iota(table_shape, 0), iota(table_shape, 1)
    target = jnp.zeros(table_shape, jnp.int32)
    for t in range(count):
        target = jnp.where(mod(col, count) == t, place[t], target)
    pack = one_hot(
        (div(mod(row, TILE), slots) == div(col, count))
        & (div(row, TILE) * slots + mod(row, slots) == target)
    )
    loads[5].wait()
    loads[6].wait()
    for c in cut_peers:
        remote(parts.at[c], parts.at[c], part_send.at[0], part_recv.at[c], (dp, c)).wait_recv()
    attn = parts[0]
    for c in range(1, n_cuts):
        attn = attn + parts[c]
    hidden = resid_ref[...].astype(F32) + attn
    hid_ref[...] = hidden
    meansq = jnp.mean(hidden * hidden, axis=1, keepdims=True)
    own = pl.ds(pl.multiple_of(cut * width, width), width)
    normed = hid_ref[:, own] * lax.rsqrt(meansq + 1e-06) * gain_ref[:, own]
    stacked = jnp.concatenate([normed[:, k * piece : (k + 1) * piece] for k in range(nq)], axis=0)
    rows = mm(pack, stacked.astype(BF16)).astype(BF16)
    packed[...] = rows.reshape(n_e, TILE, piece)

    for i, e in enumerate(e_peers):
        copy = remote(
            packed.at[e],
            gath.at[cut, g, n_e - 1 - i],
            z_send.at[i],
            z_recv.at[n_e - 1 - i],
            (e * GROUP + g, cut),
        )
        copy.start()
        sent.append(copy)
    gath[cut, g, 0] = packed[me]
    spread = (pl.ds(0, 1), pl.ds(1, n_e - 1))
    for part in range(2):
        if part == 1:
            for i, e in enumerate(e_peers):
                remote(
                    packed.at[e],
                    gath.at[cut, g, i + 1],
                    z_send.at[i],
                    z_recv.at[i + 1],
                    (e * GROUP + g, cut),
                ).wait_recv()
        block = gath.at[cut, g, spread[part]]
        for j, h in enumerate(g_peers):
            copy = remote(
                block, block, spread_send.at[part, j], spread_recv.at[part, g], (me * GROUP + h, cut)
            )
            copy.start()
            sent.append(copy)
    all_rows = GROUP * n_e * slots
    per_group = n_e * slots
    wide = GROUP * n_e * TILE
    row, col = iota((nq * all_rows, wide), 0), iota((nq * all_rows, wide), 1)
    which, m = div(row, all_rows), mod(row, all_rows)
    unpack = one_hot(col == div(m, slots) * TILE + which * slots + mod(m, slots))
    for j, h in enumerate([g] + g_peers):
        if j > 0:
            for part in range(2):
                block = gath.at[cut, h, spread[part]]
                remote(
                    block, block, spread_send.at[part, 0], spread_recv.at[part, h], (me * GROUP + h, cut)
                ).wait_recv()
        for i, c in enumerate(cut_peers):
            copy = remote(
                gath.at[cut, h], gath.at[cut, h], cross_send.at[i, j], cross_recv.at[cut, h], (dp, c)
            )
            copy.start()
            sent.append(copy)

    for load in load_up:
        load.wait()
    up = None
    for i, c in enumerate([cut] + cut_peers):
        if i > 0:
            for h in range(GROUP):
                remote(
                    gath.at[c, h], gath.at[c, h], cross_send.at[0, 0], cross_recv.at[c, h], (dp, c)
                ).wait_recv()
        arrived = mm(unpack, gath[c].reshape(wide, piece)).astype(BF16)
        arrived = jnp.concatenate(
            [arrived[k * all_rows : (k + 1) * all_rows] for k in range(nq)], axis=1
        )
        term = mm(arrived, wup_ref[pl.ds(pl.multiple_of(c * width, width), width), :])
        up = term if up is None else up + term
    act = jax.nn.gelu(up).astype(BF16)

    for load in load_down:
        load.wait()
    runs, run = share.shape[0], share.shape[3]

    def down(c, r):
        columns = pl.ds(pl.multiple_of(c * width + r * run, run), run)
        return mm(act, wdown_ref[:, columns]).astype(BF16)

    for i, c in enumerate(cut_peers):
        for r in range(runs):
            mine[c, r] = down(c, r)
            copy = remote(
                mine.at[c, r], halves.at[cut, r], half_send.at[i, r], half_recv.at[cut, r], (dp, c)
            )
            copy.start()
            sent.append(copy)
    for r in range(runs):
        summed = down(cut, r).astype(F32)
        for c in cut_peers:
            remote(
                mine.at[c, r], halves.at[c, r], half_send.at[0, r], half_recv.at[c, r], (dp, c)
            ).wait_recv()
            summed = summed + halves[c, r].astype(F32)
        share[r] = summed.astype(BF16).reshape(GROUP, per_group, run)
        for j, h in enumerate(g_peers):
            copy = remote(
                share.at[r, h], red.at[r, g], red_send.at[r, j], red_recv.at[r, g], (me * GROUP + h, cut)
            )
            copy.start()
            sent.append(copy)
    row, col = iota((n_e * TILE, nq * per_group), 0), iota((n_e * TILE, nq * per_group), 1)
    repack = one_hot(
        (div(mod(row, TILE), slots) == div(col, per_group))
        & (div(row, TILE) * slots + mod(row, slots) == mod(col, per_group))
    )
    totals = []
    for r in range(runs):
        summed = share[r, g].astype(F32)
        for h in g_peers:
            remote(
                share.at[r, h], red.at[r, h], red_send.at[r, 0], red_recv.at[r, h], (me * GROUP + h, cut)
            ).wait_recv()
            summed = summed + red[r, h].astype(F32)
        totals.append(summed)
    summed = jnp.concatenate(totals, axis=1)
    stacked = jnp.concatenate([summed[:, k * piece : (k + 1) * piece] for k in range(nq)], axis=0)
    going[...] = mm(repack, stacked.astype(BF16)).astype(BF16).reshape(n_e, TILE, piece)

    for i, e in enumerate(e_peers):
        copy = remote(
            going.at[i + 1], back.at[me], back_send.at[i], back_recv.at[me], (e * GROUP + g, cut)
        )
        copy.start()
        sent.append(copy)
    back[me] = going[0]
    table_shape = (count, n_e * TILE)
    row, col = iota(table_shape, 0), iota(table_shape, 1)
    target = jnp.zeros(table_shape, jnp.int32)
    for t in range(count):
        target = jnp.where(row == t, place[t], target)
    found = div(col, TILE) * slots + mod(col, slots) == target
    picks = [one_hot(found & (div(mod(col, TILE), slots) == k)) for k in range(nq)]
    for copy in sent:
        copy.wait_send()
    for i, e in enumerate(e_peers):
        remote(
            going.at[i + 1], back.at[e], back_send.at[i], back_recv.at[e], (e * GROUP + g, cut)
        ).wait_recv()
    returned = back[...].reshape(n_e * TILE, piece)
    expert_cols = jnp.concatenate([mm(pick, returned) for pick in picks], axis=1)
    out_ref[...] = (hid_ref[:, own] + expert_cols).astype(BF16)


def on_device(
    n_data,
    n_cuts,
    queries,
    new_keys,
    new_values,
    key_cache,
    value_cache,
    lengths,
    resid,
    norm_gain,
    w_out,
    experts,
    w_up,
    w_down,
):
    count, feats = queries.shape
    width_all = resid.shape[1]
    width = width_all // n_cuts
    n_e = n_data // GROUP
    slots = max(2, 2 * count * GROUP // n_data)
    piece = width // min(TILE // slots, width // 128)
    per_group = n_e * slots
    all_rows = GROUP * per_group
    runs = 2 if width % 256 == 0 else 1
    run = width // runs
    dma = pltpu.SemaphoreType.DMA
    hbm = pl.BlockSpec(memory_space=pltpu.HBM)
    return pl.pallas_call(
        functools.partial(kernel, n_data, n_cuts),
        out_shape=pltpu.VMEM((count, width), BF16),
        in_specs=[hbm] * 12,
        out_specs=pl.BlockSpec(memory_space=pltpu.VMEM),
        scratch_shapes=[
            pltpu.SMEM((count,), jnp.int32),
            pltpu.SMEM((count,), jnp.int32),
            pltpu.VMEM(queries.shape, BF16),
            pltpu.VMEM(new_keys.shape, BF16),
            pltpu.VMEM(new_values.shape, BF16),
            pltpu.VMEM(key_cache.shape, BF16),
            pltpu.VMEM(value_cache.shape, BF16),
            pltpu.VMEM(resid.shape, BF16),
            pltpu.VMEM((1, width_all), F32),
            pltpu.VMEM(w_out.shape, BF16),
            pltpu.VMEM(w_up.shape[1:], BF16),
            pltpu.VMEM(w_down.shape[1:], BF16),
            pltpu.VMEM((n_cuts, count, width_all), F32),
            pltpu.VMEM((count, width_all), F32),
            pltpu.VMEM((n_e, TILE, piece), BF16),
            pltpu.VMEM((n_cuts, GROUP, n_e, TILE, piece), BF16),
            pltpu.VMEM((n_cuts, runs, all_rows, run), BF16),
            pltpu.VMEM((n_cuts, runs, all_rows, run), BF16),
            pltpu.VMEM((runs, GROUP, per_group, run), BF16),
            pltpu.VMEM((runs, GROUP, per_group, run), BF16),
            pltpu.VMEM((n_e, TILE, piece), BF16),
            pltpu.VMEM((n_e, TILE, piece), BF16),
            dma((23,)),
            dma((n_cuts,)),
            dma((n_cuts,)),
            dma((n_e,)),
            dma((n_e,)),
            dma((2, GROUP)),
            dma((2, GROUP)),
            dma((n_cuts, GROUP)),
            dma((n_cuts, GROUP)),
            dma((n_cuts, runs)),
            dma((n_cuts, runs)),
            dma((runs, GROUP)),
            dma((runs, GROUP)),
            dma((n_e,)),
            dma((n_e,)),
        ],
        compiler_params=pltpu.CompilerParams(
            collective_id=0, has_side_effects=True, vmem_limit_bytes=60 * 1024 * 1024
        ),
    )(
        lengths,
        experts.reshape(count),
        queries,
        new_keys,
        new_values,
        key_cache,
        value_cache,
        resid,
        norm_gain.reshape(1, width_all),
        w_out,
        w_up,
        w_down,
    )


def solution(mesh):
    placed = (
        P("dp", "cuts"),
        P("dp", "cuts"),
        P("dp", "cuts"),
        P("dp", None, "cuts"),
        P("dp", None, "cuts"),
        P("dp"),
        P("dp", None),
        P(),
        P("cuts", None),
        P("dp", None),
        P("dp", None, "cuts"),
        P("dp", "cuts", None),
    )
    return jax.shard_map(
        functools.partial(on_device, mesh.shape["dp"], mesh.shape["cuts"]),
        mesh=mesh,
        in_specs=placed,
        out_specs=P("dp", "cuts"),
        check_vma=False,
    )
```
